256 devices in a mesh: tile: 32 (over x, z_hi, core), mode: 8 (over z_lo, y).
Axes of the slice: x: 4, y: 4, z: 8 (z_hi: 4, z_lo: 2; z = z_hi * 2 + z_lo), core: 2. Of those that a mesh axis runs over, the one named last changes fastest.
Arguments:
- object_slices: bfloat16 [3, 2, 8192, 512], P(None, None, 'tile'), may hold values from -4 to 4
- probe_modes: bfloat16 [8, 2, 256, 256], P('mode'), may hold values from -2.09375 to 2.09375
- positions: int32 [128, 2], P('tile'), may hold values from 0 to 255
- measured: float32 [128, 256, 256], P('tile'), may hold values from 0.3 to 3
Outputs:
- object_grad: float32 [3, 2, 8192, 512], P(None, None, ('tile', 'mode'))
- probe_grad: float32 [8, 2, 256, 256], P('mode')
The draws below stay inside these ranges and needn't reach their ends.
Inputs may be any that keep to these rules, and one draw needn't show every extreme that they name: `positions`: column 0 is a row offset from the top of the strip of 256 rows held by the listing tile index, column 1 a column offset; a window covers 256 x 256 cells.
All inputs are finite; a program needn't handle non-finite values.
Results may differ from the reference program's by a relative error of at most 0.035.
Values may be sent and summed in bfloat16 or wider, within the bound.
No kernel may reach another device: no remote copies, remote signals or barrier semaphores. Data moves between devices by JAX's collectives and lax.ppermute only.
A program may use at most 128 MiB of HBM per device.

```python
import math
import jax
import jax.numpy as jnp
from jax import lax

PATCH = 256
SLICES = 3
TILE_H = 256
PPD = 4
MODES = 8
OBJ_W = 512
NROWS = 8192
POSITIONS = 128


def place_ends(values, own_key, least, top_value):
    dims = values.shape
    spot = [jax.random.randint(jax.random.fold_in(own_key, axis), (), 0, dims[axis]) for axis in range(len(dims))]
    values = values.at[tuple(spot)].set(least)
    longest = dims.index(max(dims))
    spot[longest] = (spot[longest] + 1) % dims[longest]
    return values.at[tuple(spot)].set(top_value)


def shard_levels(key, dims, split, smallest, high):
    level = 1.0
    for dim, shards_of in split:
        draws = jax.random.uniform(jax.random.fold_in(jax.random.fold_in(key, 6), dim), (shards_of,), jnp.float32, smallest / len(split), high / len(split))
        level = level * jnp.repeat(jnp.exp(draws), dims[dim] // shards_of).reshape((-1,) + (1,) * (len(dims) - 1 - dim))
    return level


def noise(rng, dims, scale, reach, split=(), kind=jnp.bfloat16):
    entries = scale * jax.random.normal(rng, dims, jnp.float32)
    if split:
        entries = entries * shard_levels(rng, dims, split, -0.22, 0.18)
    return jnp.clip(entries, -reach, reach).astype(kind)


def setup_inputs(seed: int = 0) -> dict:
    arg_keys = jax.random.split(jax.random.key(seed), 5)
    object_slices = noise(arg_keys[0], (SLICES, 2, NROWS, OBJ_W), 0.7071, 4.0, ((2, 32),))
    probe_modes = noise(arg_keys[1], (MODES, 2, PATCH, PATCH), 0.35, 2.09375, ((0, 8),))
    positions = place_ends(jax.random.randint(arg_keys[2], (POSITIONS, 2), 0, TILE_H), jax.random.fold_in(arg_keys[2], 1), 0, TILE_H - 1).astype(jnp.int32)
    measured = jnp.clip(jnp.exp(math.log(3.0) - 2.3025851 * jax.random.uniform(arg_keys[3], (POSITIONS, PATCH, PATCH), jnp.float32) ** shard_levels(arg_keys[3], (POSITIONS, PATCH, PATCH), ((0, 32),), -0.2, 0.2)), 0.3, 3.0)
    return dict(object_slices=object_slices, probe_modes=probe_modes, positions=positions, measured=measured)


fresnel = 0.4

def tables(size):
    index = jnp.arange(size, dtype=jnp.int32)
    folded = index[:, None] * index[None, :] % size
    angle = 2.0 * math.pi / size * folded.astype(jnp.float32)
    scale = 1.0 / math.sqrt(size)
    table_real = (jnp.cos(angle) * scale).astype(jnp.bfloat16)
    table_imag = (-jnp.sin(angle) * scale).astype(jnp.bfloat16)
    freq = ((index + size // 2) % size - size // 2).astype(jnp.float32)
    phase = -math.pi * fresnel / size * (freq[:, None] * freq[:, None] + freq[None, :] * freq[None, :])
    return (table_real, table_imag, jnp.cos(phase), jnp.sin(phase))

def widen(value):
    return lax.optimization_barrier(value).astype(jnp.float32)

def product(first, second, form):
    return jnp.einsum(form, widen(first), widen(second))

def transform(real, imag, table_real, table_imag):
    left_form = 'jk,pkl->pjl'
    right_form = 'pjk,kl->pjl'
    mid_real = (product(table_real, real, left_form) - product(table_imag, imag, left_form)).astype(jnp.bfloat16)
    mid_imag = (product(table_real, imag, left_form) + product(table_imag, real, left_form)).astype(jnp.bfloat16)
    out_real = product(mid_real, table_real, right_form) - product(mid_imag, table_imag, right_form)
    out_imag = product(mid_real, table_imag, right_form) + product(mid_imag, table_real, right_form)
    return (out_real, out_imag)

def propagate(real, imag, tab, sign):
    table_real, table_imag, kernel_real, kernel_imag = tab
    freq_real, freq_imag = transform(real, imag, table_real, table_imag)
    turned = sign * kernel_imag
    mixed_real = (freq_real * kernel_real - freq_imag * turned).astype(jnp.bfloat16)
    mixed_imag = (freq_real * turned + freq_imag * kernel_real).astype(jnp.bfloat16)
    back_real, back_imag = transform(mixed_real, mixed_imag, table_real, -table_imag)
    return (back_real.astype(jnp.bfloat16), back_imag.astype(jnp.bfloat16))

def windows(padded, rows, columns):
    depth = padded.shape[0]
    zero = jnp.zeros((), jnp.int32)

    def single(row, column):
        return lax.dynamic_slice(padded, (zero, zero, row.astype(jnp.int32), column.astype(jnp.int32)), (depth, 2, PATCH, PATCH))
    return jax.vmap(single)(rows, columns)

def forward(probe_real, probe_imag, patches, tab):
    count = patches.shape[0]
    depth = patches.shape[1]
    wave_real = jnp.broadcast_to(probe_real, (count,) + probe_real.shape)
    wave_imag = jnp.broadcast_to(probe_imag, (count,) + probe_imag.shape)
    waves = []
    for layer in range(depth):
        obj_real = widen(patches[:, layer, 0])
        obj_imag = widen(patches[:, layer, 1])
        waves.append((wave_real, wave_imag))
        cur_real = widen(wave_real)
        cur_imag = widen(wave_imag)
        exit_real = (cur_real * obj_real - cur_imag * obj_imag).astype(jnp.bfloat16)
        exit_imag = (cur_real * obj_imag + cur_imag * obj_real).astype(jnp.bfloat16)
        if layer + 1 < depth:
            wave_real, wave_imag = propagate(exit_real, exit_imag, tab, 1.0)
    far_real, far_imag = transform(exit_real, exit_imag, tab[0], tab[1])
    return (waves, far_real, far_imag)

def backward(waves, far_real, far_imag, residual, patches, tab):
    depth = patches.shape[1]
    grad_real = (residual * far_real).astype(jnp.bfloat16)
    grad_imag = (residual * far_imag).astype(jnp.bfloat16)
    back_real, back_imag = transform(grad_real, grad_imag, tab[0], -tab[1])
    back_real = back_real.astype(jnp.bfloat16)
    back_imag = back_imag.astype(jnp.bfloat16)
    pieces = [None] * depth
    probe_piece = None
    for layer in reversed(range(depth)):
        cur_real = widen(waves[layer][0])
        cur_imag = widen(waves[layer][1])
        obj_real = widen(patches[:, layer, 0])
        obj_imag = widen(patches[:, layer, 1])
        gin_real = widen(back_real)
        gin_imag = widen(back_imag)
        pieces[layer] = jnp.stack([cur_real * gin_real + cur_imag * gin_imag, cur_real * gin_imag - cur_imag * gin_real], axis=1)
        wave_grad_real = obj_real * gin_real + obj_imag * gin_imag
        wave_grad_imag = obj_real * gin_imag - obj_imag * gin_real
        if layer > 0:
            back_real, back_imag = propagate(wave_grad_real.astype(jnp.bfloat16), wave_grad_imag.astype(jnp.bfloat16), tab, -1.0)
        else:
            probe_piece = jnp.stack([lax.optimization_barrier(jnp.sum(wave_grad_real, axis=0)), lax.optimization_barrier(jnp.sum(wave_grad_imag, axis=0))])
    return (jnp.stack(pieces, axis=1), probe_piece)

def reference(object_slices, probe_modes, positions, measured):
    tab = tables(PATCH)
    padded = jnp.concatenate([object_slices, object_slices[:, :, :TILE_H]], axis=2)
    owner = jnp.arange(POSITIONS, dtype=jnp.int32) // PPD * TILE_H
    rows = (owner + positions[:, 0]).astype(jnp.int32)
    columns = positions[:, 1].astype(jnp.int32)
    patches = windows(padded, rows, columns)

    def intensity_step(total, probe):
        waves, far_real, far_imag = forward(probe[0], probe[1], patches, tab)
        return (total + far_real * far_real + far_imag * far_imag, None)
    intensity, _ = lax.scan(intensity_step, jnp.zeros((POSITIONS, PATCH, PATCH), jnp.float32), probe_modes)
    residual = intensity - measured

    def grad_step(total, probe):
        waves, far_real, far_imag = forward(probe[0], probe[1], patches, tab)
        pieces, probe_piece = backward(waves, far_real, far_imag, residual, patches, tab)
        return (total + pieces, probe_piece)
    start_sum = jnp.zeros((POSITIONS, SLICES, 2, PATCH, PATCH), jnp.float32)
    pieces, probe_grad = lax.scan(grad_step, start_sum, probe_modes)
    zero = jnp.zeros((), jnp.int32)

    def place(index, total):
        begin = (zero, zero, rows[index], columns[index])
        current = lax.dynamic_slice(total, begin, (SLICES, 2, PATCH, PATCH))
        return lax.dynamic_update_slice(total, current + pieces[index], begin)
    grad = lax.fori_loop(0, POSITIONS, place, jnp.zeros(padded.shape, jnp.float32))
    object_grad = grad[:, :, :NROWS].at[:, :, :TILE_H].add(grad[:, :, NROWS:])
    return (object_grad, probe_grad)
```

```python
import functools
import math

import jax
import jax.numpy as jnp
import numpy as np
from jax import lax
from jax.experimental import pallas as pl
from jax.experimental.pallas import tpu as pltpu
from jax.sharding import PartitionSpec as P

fresnel = 0.4
SIDE = 256
DEPTH = 3
SLOTS = 4
BF = jnp.bfloat16
F32 = jnp.float32
VMEM = pl.BlockSpec(memory_space=pltpu.VMEM)
SMEM = pl.BlockSpec(memory_space=pltpu.SMEM)
PARAMS = pltpu.CompilerParams(vmem_limit_bytes=48 * 1024 * 1024)


def constants():
    index = np.arange(SIDE)
    folded = index[:, None] * index[None, :] % SIDE
    angle = np.float32(2.0 * math.pi / SIDE) * folded.astype(np.float32)
    scale = np.float32(1.0 / math.sqrt(SIDE))
    real = (np.cos(angle) * scale).astype(jnp.bfloat16)
    imag = (-np.sin(angle) * scale).astype(jnp.bfloat16)
    table = np.block([[real, imag], [-imag, real]])
    freq = ((index + SIDE // 2) % SIDE - SIDE // 2).astype(np.float64)
    phase = -math.pi * fresnel / SIDE * (freq[:, None] ** 2 + freq[None, :] ** 2)
    kernel = np.stack([np.cos(phase), np.sin(phase)]).astype(np.float32)
    return table, kernel


def swap(block, axis, bits):
    route = [(i, i ^ bits) for i in range(lax.axis_size(axis))]
    return lax.ppermute(block, axis, route)


def shift(block, axis, distance):
    size = lax.axis_size(axis)
    return lax.ppermute(block, axis, [(i, (i + distance) % size) for i in range(size)])


def dot(first, second):
    return jnp.dot(first, second, preferred_element_type=F32)


def iotas():
    rows = lax.broadcasted_iota(jnp.int32, (SIDE, SIDE), 0)
    cols = lax.broadcasted_iota(jnp.int32, (SIDE, SIDE), 1)
    return rows, cols


def to_residues(offset):
    rows, cols = iotas()
    return jnp.where(((rows - offset) & (SIDE - 1)) == cols, 1.0, 0.0).astype(BF)


def from_residues(offset):
    rows, cols = iotas()
    return jnp.where(((cols - offset) & (SIDE - 1)) == rows, 1.0, 0.0).astype(BF)


def prepare_kernel(pos_ref, table_ref, table_t_ref, probe0, probe1, probe2, probe3, *outs):
    row_t, row_tt, col_t, col_tt, probe_out = outs
    for axis, plain, turned in ((0, row_t, row_tt), (1, col_t, col_tt)):
        offset = pos_ref[axis]
        there = to_residues(offset)
        back = from_residues(offset)
        for half in range(2):
            part = pl.ds(half * SIDE, SIDE)
            plain[part, :] = dot(there, table_ref[part, :]).astype(BF)
            turned[:, part] = dot(table_t_ref[:, part], back).astype(BF)
    rows = to_residues(pos_ref[0])
    cols = from_residues(pos_ref[1])
    for slot, probe in enumerate((probe0, probe1, probe2, probe3)):
        for part in range(2):
            moved = dot(rows, probe[part]).astype(BF)
            probe_out[slot, part] = dot(moved, cols).astype(BF)


def fill(field, slot, real, imag):
    field[slot, :SIDE, :] = real.astype(BF)
    field[slot, SIDE:, :] = imag.astype(BF)


def transform(field, mid, slot, left, right):
    turned = dot(left[...], field[slot])
    mid[slot, :, :SIDE] = turned[:SIDE].astype(BF)
    mid[slot, :, SIDE:] = turned[SIDE:].astype(BF)
    out = dot(mid[slot], right[...])
    return out[:, :SIDE], out[:, SIDE:]


def propagate(field, mid, slot, forth, back, kernel, sign):
    real, imag = transform(field, mid, slot, *forth)
    kernel_real = kernel[0]
    turned = sign * kernel[1]
    fill(field, slot, real * kernel_real - imag * turned, real * turned + imag * kernel_real)
    return transform(field, mid, slot, *back)


def forward_kernel(
    pos_ref, own, halo, probes, row_t, row_tt, col_t, col_tt, kernel,
    window, wave1, wave2, far, total, total_sent, field, mid,
):
    rows, cols = iotas()
    on_left = cols >= pos_ref[1]
    on_strip = rows >= pos_ref[0]
    for layer in range(DEPTH):
        for part in range(2):
            strip = own[layer, part].astype(F32)
            picked = jnp.where(on_left, strip[:, :SIDE], strip[:, SIDE:])
            below = halo[layer, part].astype(F32)
            window[layer, part] = jnp.where(on_strip, picked, below).astype(BF)
    forth = (row_tt, col_t)
    back = (row_t, col_tt)
    waves = (probes, wave1, wave2)
    for layer in range(DEPTH):
        for slot in range(SLOTS):
            obj_real = window[layer, 0].astype(F32)
            obj_imag = window[layer, 1].astype(F32)
            real = waves[layer][slot, 0].astype(F32)
            imag = waves[layer][slot, 1].astype(F32)
            fill(field, slot, real * obj_real - imag * obj_imag, real * obj_imag + imag * obj_real)
            if layer + 1 < DEPTH:
                real, imag = propagate(field, mid, slot, forth, back, kernel, 1.0)
                waves[layer + 1][slot, 0] = real.astype(BF)
                waves[layer + 1][slot, 1] = imag.astype(BF)
            else:
                real, imag = transform(field, mid, slot, *forth)
                far[slot, 0] = real
                far[slot, 1] = imag
                power = real * real + imag * imag
                total[...] = power if slot == 0 else total[...] + power
    total_sent[...] = total[...].astype(BF)


def backward_kernel(
    pos_ref, which_ref, window, probes, wave1, wave2, far, total, total_got, measured,
    row_t, row_tt, col_t, col_tt, kernel,
    grad_out, keep_out, send_out, field, mid, residual, grads, pieces,
):
    residual[...] = total[...] + total_got[...].astype(F32) - measured[0]
    forth = (row_tt, col_t)
    back = (row_t, col_tt)
    waves = (probes, wave1, wave2)
    rows = from_residues(pos_ref[0])
    cols = to_residues(pos_ref[1])
    backs = [None] * SLOTS
    for slot in range(SLOTS):
        fill(field, slot, residual[...] * far[slot, 0], residual[...] * far[slot, 1])
        backs[slot] = transform(field, mid, slot, *back)
    for layer in reversed(range(DEPTH)):
        for slot in range(SLOTS):
            gin_real, gin_imag = (part.astype(BF).astype(F32) for part in backs[slot])
            real = waves[layer][slot, 0].astype(F32)
            imag = waves[layer][slot, 1].astype(F32)
            grad_real = real * gin_real + imag * gin_imag
            grad_imag = real * gin_imag - imag * gin_real
            if slot > 0:
                grad_real += grads[0]
                grad_imag += grads[1]
            if slot + 1 < SLOTS:
                grads[0] = grad_real
                grads[1] = grad_imag
            else:
                shape = (8, SIDE // 8, SIDE)
                grad_out[:, layer, 0] = grad_real.astype(BF).reshape(shape)
                grad_out[:, layer, 1] = grad_imag.astype(BF).reshape(shape)
            obj_real = window[layer, 0].astype(F32)
            obj_imag = window[layer, 1].astype(F32)
            next_real = obj_real * gin_real + obj_imag * gin_imag
            next_imag = obj_real * gin_imag - obj_imag * gin_real
            if layer > 0:
                fill(field, slot, next_real, next_imag)
                backs[slot] = propagate(field, mid, slot, forth, back, kernel, -1.0)
            else:
                for part, value in enumerate((next_real, next_imag)):
                    moved = dot(rows, value.astype(BF)).astype(BF)
                    pieces[slot, part] = dot(moved, cols).astype(BF)
    half = SIDE // 2
    kept = which_ref[1]
    keep_out[...] = pieces[:, :, pl.ds(kept * half, half), :]
    send_out[...] = pieces[:, :, pl.ds((1 - kept) * half, half), :]


def gather_kernel(which_ref, positions, grads, own_out, spill_out):
    band = SIDE // 8
    top = which_ref[0] * band
    shape = (band, SIDE)
    rows = lax.broadcasted_iota(jnp.int32, shape, 0) + top
    cols = lax.broadcasted_iota(jnp.int32, shape, 1)
    for layer in range(DEPTH):
        for part in range(2):
            sums = [jnp.zeros(shape, F32) for _ in range(4)]
            for place in range(SLOTS):
                value = grads[place, layer, part].astype(F32)
                value += grads[SLOTS + place, layer, part].astype(F32)
                on_strip = rows >= positions[place, 0]
                on_left = cols >= positions[place, 1]
                for index, (here, left) in enumerate(
                    ((True, True), (True, False), (False, True), (False, False))
                ):
                    picked = on_strip if here else ~on_strip
                    picked &= on_left if left else ~on_left
                    sums[index] += jnp.where(picked, value, 0.0)
            own_out[layer, part, :, :SIDE] = sums[0]
            own_out[layer, part, :, SIDE:] = sums[1]
            spill_out[layer, part, :, :SIDE] = sums[2].astype(BF)
            spill_out[layer, part, :, SIDE:] = sums[3].astype(BF)


def quarter_kernel(which_ref, own, got1, got2, got3, *outs):
    total = own[...].astype(F32) + got1[...].astype(F32)
    total += got2[...].astype(F32) + got3[...].astype(F32)
    held = total.astype(BF)
    depth = held.shape[1] // 4
    scratch = outs[-1]
    scratch[...] = held
    for step in range(4):
        outs[step][...] = scratch[:, pl.ds((which_ref[2] ^ step) * depth, depth), :]


def merge_kernel(which_ref, part0, part1, part2, part3, out):
    depth = part0.shape[1]
    for step, part in enumerate((part0, part1, part2, part3)):
        out[:, pl.ds((which_ref[2] ^ step) * depth, depth), :] = part[...]


def finish_kernel(which_ref, own, got, out):
    half = SIDE // 2
    kept = which_ref[1]
    out[0, :, pl.ds(kept * half, half), :] = own[...].astype(F32)
    out[0, :, pl.ds((1 - kept) * half, half), :] = got[...].astype(F32)


def call(kernel, outs, arguments, scalars, scratch=()):
    return pl.pallas_call(
        kernel,
        out_shape=[jax.ShapeDtypeStruct(shape, dtype) for shape, dtype in outs],
        in_specs=[SMEM] * scalars + [VMEM] * (len(arguments) - scalars),
        out_specs=[VMEM] * len(outs),
        scratch_shapes=[pltpu.VMEM(shape, dtype) for shape, dtype in scratch],
        compiler_params=PARAMS,
    )(*arguments)


def on_device(object_slices, probe_modes, positions, measured):
    tile = lax.axis_index("tile")
    mode = lax.axis_index("mode")
    place = mode & (SLOTS - 1)
    half = SIDE // 2
    square = (SIDE, SIDE)
    table, kernel = constants()
    table_t = jnp.asarray(table.T)
    table = jnp.asarray(table)
    kernel = jnp.asarray(kernel)
    which = jnp.stack([mode, tile & 1, tile >> 3, place]).astype(jnp.int32)

    pos = lax.dynamic_index_in_dim(positions, place, 0, keepdims=False)
    above = shift(pos, "tile", 1)
    columns = lax.broadcasted_iota(jnp.int32, square, 1)
    chosen = jnp.where(columns >= above[1], object_slices[..., :SIDE], object_slices[..., SIDE:])
    halo = shift(chosen, "tile", -1)
    probes = [probe_modes[0]] + [swap(probe_modes[0], "mode", step) for step in range(1, 4)]

    wide = (2 * SIDE, 2 * SIDE)
    tables = call(
        prepare_kernel,
        [(wide, BF)] * 4 + [((SLOTS, 2) + square, BF)],
        (pos, table, table_t, *probes),
        1,
    )
    tables, rolled = tables[:4], tables[4]
    scratch = [((SLOTS, 2 * SIDE, SIDE), BF), ((SLOTS, SIDE, 2 * SIDE), BF)]
    window, wave1, wave2, far, total, total_sent = call(
        forward_kernel,
        [
            ((DEPTH, 2) + square, BF),
            ((SLOTS, 2) + square, BF),
            ((SLOTS, 2) + square, BF),
            ((SLOTS, 2) + square, F32),
            (square, F32),
            (square, BF),
        ],
        (pos, object_slices, halo, rolled, *tables, kernel),
        1,
        scratch,
    )
    total_got = swap(total_sent, "mode", 4)
    picked = lax.dynamic_index_in_dim(measured, place, 0, keepdims=True)
    grads, keep, send = call(
        backward_kernel,
        [
            ((8, DEPTH, 2, SIDE // 8, SIDE), BF),
            ((SLOTS, 2, half, SIDE), BF),
            ((SLOTS, 2, half, SIDE), BF),
        ],
        (pos, which, window, rolled, wave1, wave2, far, total, total_got, picked, *tables, kernel),
        2,
        scratch + [(square, F32), ((2,) + square, F32), ((SLOTS, 2) + square, BF)],
    )

    got = swap(send, "tile", 1)
    summed = (keep.astype(F32) + got.astype(F32)).astype(BF)
    parts = [summed[0]] + [swap(summed[step], "mode", step) for step in range(1, 4)]
    quarter = (2, half // 4, SIDE)
    quarters = call(
        quarter_kernel, [(quarter, BF)] * 4, (which, *parts), 1, [((2, half, SIDE), BF)]
    )
    parts = [quarters[0]] + [swap(quarters[step], "tile", step << 3) for step in range(1, 4)]
    part = ((parts[0].astype(F32) + parts[1]) + (parts[2].astype(F32) + parts[3])).astype(BF)
    parts = [part] + [swap(part, "tile", step << 1) for step in range(1, 4)]
    part = ((parts[0].astype(F32) + parts[1]) + (parts[2].astype(F32) + parts[3])).astype(BF)
    parts = [part] + [swap(part, "tile", step << 3) for step in range(1, 4)]
    (merged,) = call(merge_kernel, [((2, half, SIDE), BF)], (which, *parts), 1)
    (probe_grad,) = call(
        finish_kernel, [((1, 2) + square, F32)], (which, merged, swap(merged, "tile", 1)), 1
    )

    bands = lax.all_to_all(grads, "mode", 0, 0, tiled=True)
    shape = (DEPTH, 2, SIDE // 8, 2 * SIDE)
    own, spill = call(gather_kernel, [(shape, F32), (shape, BF)], (which, positions, bands), 2)
    object_grad = own + shift(spill, "tile", 1).astype(F32)
    return (object_grad, probe_grad)


def solution(mesh):
    placed = (
        P(None, None, "tile", None),
        P("mode", None, None, None),
        P("tile", None),
        P("tile", None, None),
    )
    return jax.shard_map(
        on_device,
        mesh=mesh,
        in_specs=placed,
        out_specs=(P(None, None, ("tile", "mode"), None), P("mode", None, None, None)),
        check_vma=False,
    )
```

```python
import math

import jax
import jax.numpy as jnp
import numpy as np
from jax import lax
from jax.experimental import pallas as pl
from jax.experimental.pallas import tpu as pltpu
from jax.sharding import PartitionSpec as P

fresnel = 0.4
SIDE = 256
DEPTH = 3
SLOTS = 4
BF = jnp.bfloat16
F32 = jnp.float32
VMEM = pl.BlockSpec(memory_space=pltpu.VMEM)
HBM = pl.BlockSpec(memory_space=pltpu.HBM)
SMEM = pl.BlockSpec(memory_space=pltpu.SMEM)
PARAMS = pltpu.CompilerParams(vmem_limit_bytes=16 * 1024 * 1024)


def constants():
    index = np.arange(SIDE)
    folded = index[:, None] * index[None, :] % SIDE
    angle = np.float32(2.0 * math.pi / SIDE) * folded.astype(np.float32)
    scale = np.float32(1.0 / math.sqrt(SIDE))
    real = (np.cos(angle) * scale).astype(jnp.bfloat16)
    imag = (-np.sin(angle) * scale).astype(jnp.bfloat16)
    return np.concatenate([real, imag], 1)


def swap(block, axis, bits):
    route = [(i, i ^ bits) for i in range(lax.axis_size(axis))]
    return lax.ppermute(block, axis, route)


def shift(block, axis, distance):
    size = lax.axis_size(axis)
    return lax.ppermute(block, axis, [(i, (i + distance) % size) for i in range(size)])


def dot(first, second):
    return jnp.dot(first, second, preferred_element_type=F32)


def row_of(which, place):
    return which[4 + 2 * place]


def column_of(which, place):
    return which[5 + 2 * place]


def iotas():
    rows = lax.broadcasted_iota(jnp.int32, (SIDE, SIDE), 0)
    cols = lax.broadcasted_iota(jnp.int32, (SIDE, SIDE), 1)
    return rows, cols


def to_residues(offset):
    rows, cols = iotas()
    return jnp.where(((rows - offset) & (SIDE - 1)) == cols, 1.0, 0.0).astype(BF)


def from_residues(offset):
    rows, cols = iotas()
    return jnp.where(((cols - offset) & (SIDE - 1)) == rows, 1.0, 0.0).astype(BF)


def make_tables(which, table, row_t, row_tt, col_t, col_tt, kernel):
    place = which[1]
    offsets = (row_of(which, place), column_of(which, place))
    for offset, plain, turned in zip(offsets, (row_t, col_t), (row_tt, col_tt)):
        rolled = dot(to_residues(offset), table[...]).astype(BF)
        real, imag = rolled[:, :SIDE], rolled[:, SIDE:]
        plain[:SIDE, :SIDE] = real
        plain[:SIDE, SIDE:] = imag
        plain[SIDE:, :SIDE] = -imag
        plain[SIDE:, SIDE:] = real
        back = from_residues(offset)
        real = dot(table[:, :SIDE], back).astype(BF)
        imag = dot(table[:, SIDE:], back).astype(BF)
        turned[:SIDE, :SIDE] = real
        turned[:SIDE, SIDE:] = -imag
        turned[SIDE:, :SIDE] = imag
        turned[SIDE:, SIDE:] = real
    index = lax.broadcasted_iota(jnp.int32, (8, SIDE), 1)
    freq = (((index + SIDE // 2) & (SIDE - 1)) - SIDE // 2).astype(F32)
    phase = freq * freq * (-math.pi * fresnel / SIDE)
    cos_row = jnp.broadcast_to(jnp.cos(phase)[:1], (SIDE, SIDE))
    sin_row = jnp.broadcast_to(jnp.sin(phase)[:1], (SIDE, SIDE))
    cos_col, sin_col = cos_row.T, sin_row.T
    kernel[0] = cos_col * cos_row - sin_col * sin_row
    kernel[1] = cos_col * sin_row + sin_col * cos_row


def fill(field, slot, real, imag):
    field[slot, :SIDE, :] = real.astype(BF)
    field[slot, SIDE:, :] = imag.astype(BF)


def transform(field, mid, slot, left, right):
    turned = dot(left[...], field[slot])
    mid[slot, :, :SIDE] = turned[:SIDE].astype(BF)
    mid[slot, :, SIDE:] = turned[SIDE:].astype(BF)
    out = dot(mid[slot], right[...])
    return out[:, :SIDE], out[:, SIDE:]


def transform_all(field, mid, slots, left, right, store):
    for slot in range(slots):
        store(slot, *transform(field, mid, slot, left, right))


def propagate_all(field, mid, slots, forth, back, kernel, sign, store):
    def turn(slot, real, imag):
        turned = sign * kernel[1]
        fill(field, slot, real * kernel[0] - imag * turned, real * turned + imag * kernel[0])

    transform_all(field, mid, slots, *forth, turn)
    transform_all(field, mid, slots, *back, store)


def choose_kernel(which, above, strip, out):
    cols = lax.broadcasted_iota(jnp.int32, (SIDE, SIDE), 1)
    on_left = cols >= above[which[1], 1]
    part = which[0] >> 2
    for layer in range(DEPTH):
        value = strip[layer, part].astype(F32)
        out[layer] = jnp.where(on_left, value[:, :SIDE], value[:, SIDE:]).astype(BF)


def forward_kernel(which, strip_hbm, *refs):
    mine, other, *probes_hbm = refs[:7]
    table, window, wave0, wave1, wave2, far, total, total_sent, *refs = refs[7:]
    row_t, row_tt, col_t, col_tt, kernel, field, mid, own, probes, sem = refs
    copies = [pltpu.make_async_copy(strip_hbm, own, sem.at[0])]
    places = (probes.at[0], probes.at[1], probes.at[2, 0], probes.at[2, 1], probes.at[3])
    for index, (source, target) in enumerate(zip(probes_hbm, places)):
        copies.append(pltpu.make_async_copy(source, target, sem.at[index + 1]))
    for copy in copies:
        copy.start()
    mode, place = which[0], which[1]
    row, col = row_of(which, place), column_of(which, place)
    make_tables(which, table, row_t, row_tt, col_t, col_tt, kernel)
    there = to_residues(row)
    back = from_residues(col)
    for copy in copies:
        copy.wait()
    for slot in range(SLOTS):
        for part in range(2):
            moved = dot(there, probes[slot, part]).astype(BF)
            wave0[slot, part] = dot(moved, back).astype(BF)
    rows, cols = iotas()
    on_left = cols >= col
    on_strip = rows >= row
    for layer in range(DEPTH):
        for part in range(2):
            strip = own[layer, part].astype(F32)
            picked = jnp.where(on_left, strip[:, :SIDE], strip[:, SIDE:])
            have = (mode >> 2) == part
            below = jnp.where(have, mine[layer].astype(F32), other[layer].astype(F32))
            window[layer, part] = jnp.where(on_strip, picked, below).astype(BF)
    forth = (row_tt, col_t)
    back = (row_t, col_tt)
    waves = (wave0, wave1, wave2)

    def store_far(slot, real, imag):
        far[slot, 0] = real
        far[slot, 1] = imag
        power = real * real + imag * imag
        total[...] = power if slot == 0 else total[...] + power

    for layer in range(DEPTH):
        for slot in range(SLOTS):
            obj_real = window[layer, 0].astype(F32)
            obj_imag = window[layer, 1].astype(F32)
            real = waves[layer][slot, 0].astype(F32)
            imag = waves[layer][slot, 1].astype(F32)
            fill(field, slot, real * obj_real - imag * obj_imag, real * obj_imag + imag * obj_real)
        if layer + 1 < DEPTH:

            def store(slot, real, imag, wave=waves[layer + 1]):
                wave[slot, 0] = real.astype(BF)
                wave[slot, 1] = imag.astype(BF)

            propagate_all(field, mid, SLOTS, forth, back, kernel, 1.0, store)
        else:
            transform_all(field, mid, SLOTS, *forth, store_far)
    total_sent[...] = total[...].astype(BF)


def backward_kernel(
    which, window, wave0, wave1, wave2, far, total, total_got, measured_hbm,
    table,
    grad_keep, grad_send, keep_out, send_out,
    row_t, row_tt, col_t, col_tt, kernel, field, mid, residual, grads, sums, backs, measured, sem,
):
    place = which[1]
    copy = pltpu.make_async_copy(measured_hbm.at[place], measured, sem)
    copy.start()
    row, col = row_of(which, place), column_of(which, place)
    make_tables(which, table, row_t, row_tt, col_t, col_tt, kernel)
    copy.wait()
    residual[...] = total[...] + total_got[...].astype(F32) - measured[...]
    forth = (row_tt, col_t)
    back = (row_t, col_tt)
    waves = (wave0, wave1, wave2)

    def store(slot, real, imag):
        backs[slot, 0] = real.astype(BF)
        backs[slot, 1] = imag.astype(BF)

    for slot in range(SLOTS):
        fill(field, slot, residual[...] * far[slot, 0], residual[...] * far[slot, 1])
    transform_all(field, mid, SLOTS, *back, store)
    for layer in reversed(range(DEPTH)):
        for slot in range(SLOTS):
            gin_real = backs[slot, 0].astype(F32)
            gin_imag = backs[slot, 1].astype(F32)
            real = waves[layer][slot, 0].astype(F32)
            imag = waves[layer][slot, 1].astype(F32)
            grad_real = real * gin_real + imag * gin_imag
            grad_imag = real * gin_imag - imag * gin_real
            if slot > 0:
                grad_real += grads[0]
                grad_imag += grads[1]
            if slot + 1 < SLOTS:
                grads[0] = grad_real
                grads[1] = grad_imag
            else:
                sums[layer, 0] = grad_real.astype(BF)
                sums[layer, 1] = grad_imag.astype(BF)
            obj_real = window[layer, 0].astype(F32)
            obj_imag = window[layer, 1].astype(F32)
            next_real = obj_real * gin_real + obj_imag * gin_imag
            next_imag = obj_real * gin_imag - obj_imag * gin_real
            fill(field, slot, next_real, next_imag)
        if layer > 0:
            propagate_all(field, mid, SLOTS, forth, back, kernel, -1.0, store)
    rows = from_residues(row)
    cols = to_residues(col)
    for slot in range(SLOTS):
        for part in range(2):
            moved = dot(rows, field[slot, part * SIDE : (part + 1) * SIDE, :]).astype(BF)
            backs[slot, part] = dot(moved, cols).astype(BF)
    half = SIDE // 2
    kept = pl.multiple_of((which[0] >> 2) * half, half)
    sent = pl.multiple_of(half - kept, half)
    grad_keep[...] = sums[:, :, pl.ds(kept, half), :]
    grad_send[...] = sums[:, :, pl.ds(sent, half), :]
    kept = pl.multiple_of(which[2] * half, half)
    sent = pl.multiple_of(half - kept, half)
    keep_out[...] = backs[:, :, pl.ds(kept, half), :]
    send_out[...] = backs[:, :, pl.ds(sent, half), :]


def pair_kernel(which, keep, got, own_out, *outs):
    band = SIDE // 8
    for step in range(SLOTS):
        part = pl.ds(pl.multiple_of((which[1] ^ step) * band, band), band)
        for layer in range(DEPTH):
            for side in range(2):
                value = keep[layer, side, part, :].astype(F32) + got[layer, side, part, :].astype(F32)
                if step == 0:
                    own_out[layer, side] = value
                else:
                    outs[step - 1][layer, side] = value.astype(BF)


def gather_kernel(which, own, got1, got2, got3, own_out, spill_out):
    band = SIDE // 8
    top = which[0] * band
    shape = (band, SIDE)
    rows = lax.broadcasted_iota(jnp.int32, shape, 0) + top
    cols = lax.broadcasted_iota(jnp.int32, shape, 1)
    for layer in range(DEPTH):
        for part in range(2):
            sums = [jnp.zeros(shape, F32) for _ in range(4)]
            for step, grads in enumerate((own, got1, got2, got3)):
                value = grads[layer, part].astype(F32)
                place = which[1] ^ step
                on_strip = rows >= row_of(which, place)
                on_left = cols >= column_of(which, place)
                for index, (here, left) in enumerate(
                    ((True, True), (True, False), (False, True), (False, False))
                ):
                    picked = on_strip if here else ~on_strip
                    picked &= on_left if left else ~on_left
                    sums[index] += jnp.where(picked, value, 0.0)
            own_out[layer, part, :, :SIDE] = sums[0]
            own_out[layer, part, :, SIDE:] = sums[1]
            spill_out[layer, part, :, :SIDE] = sums[2].astype(BF)
            spill_out[layer, part, :, SIDE:] = sums[3].astype(BF)


def first_kernel(keep, got, own, sent_one, sent_three):
    for slot in range(SLOTS):
        for part in range(2):
            total = (keep[slot, part].astype(F32) + got[slot, part].astype(F32)).astype(BF)
            if part == 0 and slot in (1, 2):
                sent_one[slot - 1] = total
            elif part == 1 and slot in (2, 3):
                sent_three[3 - slot] = total
            else:
                own[slot if slot == 0 else 1, part] = total


def second_kernel(own, got_one, got_three, held, sent_three, sent_one):
    for part, got, sent in ((0, got_one, sent_three), (1, got_three, sent_one)):
        held[part] = own[0, part].astype(F32) + got[0].astype(F32)
        sent[...] = (own[1, part].astype(F32) + got[1].astype(F32)).astype(BF)


def quarter_kernel(which, held, got_three, got_one, *outs):
    scratch = outs[-1]
    scratch[0] = (held[0] + got_three[...].astype(F32)).astype(BF)
    scratch[1] = (held[1] + got_one[...].astype(F32)).astype(BF)
    depth = scratch.shape[1] // 4
    for step in range(4):
        top = pl.multiple_of((which[3] ^ step) * depth, depth)
        outs[step][...] = scratch[:, pl.ds(top, depth), :]


def merge_kernel(which, part0, part1, part2, part3, out):
    depth = part0.shape[1]
    for step, part in enumerate((part0, part1, part2, part3)):
        top = pl.multiple_of((which[3] ^ step) * depth, depth)
        out[:, pl.ds(top, depth), :] = part[...]


def finish_kernel(which, own, got, out):
    half = SIDE // 2
    kept = pl.multiple_of(which[2] * half, half)
    out[0, :, pl.ds(kept, half), :] = own[...].astype(F32)
    out[0, :, pl.ds(pl.multiple_of(half - kept, half), half), :] = got[...].astype(F32)


def call(kernel, outs, arguments, scalars, scratch=()):
    return pl.pallas_call(
        kernel,
        out_shape=[jax.ShapeDtypeStruct(shape, dtype) for shape, dtype in outs],
        in_specs=[SMEM] * scalars + [VMEM] * (len(arguments) - scalars),
        out_specs=[VMEM] * len(outs),
        scratch_shapes=[pltpu.VMEM(shape, dtype) for shape, dtype in scratch],
        compiler_params=PARAMS,
    )(*arguments)


def on_device(object_slices, probe_modes, positions, measured):
    tile = lax.axis_index("tile")
    mode = lax.axis_index("mode")
    place = mode & (SLOTS - 1)
    which = jnp.stack([mode, place, tile & 1, tile >> 3]).astype(jnp.int32)
    which = jnp.concatenate([which, positions.reshape(-1)])
    half = SIDE // 2
    band = SIDE // 8
    square = (SIDE, SIDE)
    wide = (2 * SIDE, 2 * SIDE)
    table = jnp.asarray(constants())

    above = shift(positions, "tile", 1)
    (chosen,) = call(choose_kernel, [((DEPTH,) + square, BF)], (which, above, object_slices), 2)
    mine = shift(chosen, "tile", -1)
    one, three = (swap(probe_modes[0], "mode", step) for step in (1, 3))
    two = [swap(three[0], "mode", 1), swap(one[1], "mode", 3)]
    other = swap(mine, "mode", 4)

    slots = (SLOTS, 2) + square
    layers = (DEPTH, 2) + square
    scratch = [(wide, BF)] * 4 + [((2,) + square, F32)]
    scratch += [((SLOTS, 2 * SIDE, SIDE), BF), ((SLOTS, SIDE, 2 * SIDE), BF)]
    outs = [(layers, BF)] + [(slots, BF)] * 3 + [(slots, F32), (square, F32), (square, BF)]
    window, wave0, wave1, wave2, far, total, total_sent = pl.pallas_call(
        forward_kernel,
        out_shape=[jax.ShapeDtypeStruct(*out) for out in outs],
        in_specs=[SMEM, HBM] + [VMEM] * 2 + [HBM] * 5 + [VMEM],
        out_specs=[VMEM] * 7,
        scratch_shapes=[
            pltpu.VMEM(*shape)
            for shape in scratch + [((DEPTH, 2, SIDE, 2 * SIDE), BF), (slots, BF)]
        ]
        + [pltpu.SemaphoreType.DMA((6,))],
        compiler_params=PARAMS,
    )(which, object_slices, mine, other, probe_modes[0], one, *two, three, table)
    total_got = swap(total_sent, "mode", 4)
    piece = ((SLOTS, 2, half, SIDE), BF)
    outs = [((DEPTH, 2, half, SIDE), BF)] * 2 + [piece, piece]
    scratch += [(square, F32), ((2,) + square, F32), (layers, BF), (slots, BF), (square, F32)]
    grad_keep, grad_send, keep, send = pl.pallas_call(
        backward_kernel,
        out_shape=[jax.ShapeDtypeStruct(*out) for out in outs],
        in_specs=[SMEM] + [VMEM] * 7 + [HBM, VMEM],
        out_specs=[VMEM] * 4,
        scratch_shapes=[pltpu.VMEM(*shape) for shape in scratch] + [pltpu.SemaphoreType.DMA],
        compiler_params=PARAMS,
    )(which, window, wave0, wave1, wave2, far, total, total_got, measured, table)

    grad_got = swap(grad_send, "mode", 4)

    pair = ((2, half, SIDE), BF)
    own, sent_one, sent_three = call(
        first_kernel, [((2,) + pair[0], BF), pair, pair], (keep, swap(send, "tile", 1)), 0
    )
    held, sent_three, sent_one = call(
        second_kernel,
        [(pair[0], F32), ((half, SIDE), BF), ((half, SIDE), BF)],
        (own, swap(sent_one, "mode", 1), swap(sent_three, "mode", 3)),
        0,
    )
    quarters = call(
        quarter_kernel,
        [((2, half // 4, SIDE), BF)] * 4,
        (which, held, swap(sent_three, "mode", 3), swap(sent_one, "mode", 1)),
        1,
        [pair],
    )
    parts = [quarters[0]] + [swap(quarters[step], "tile", step << 3) for step in range(1, 4)]
    grad_got, quarters = lax.optimization_barrier((grad_got, quarters))
    shape = (DEPTH, 2, band, SIDE)
    bands = call(
        pair_kernel, [(shape, F32)] + [(shape, BF)] * 3, (which, grad_keep, grad_got), 1
    )
    bands, parts = lax.optimization_barrier((bands, parts))
    bands = [bands[0]] + [swap(bands[step], "mode", step) for step in range(1, 4)]
    part = ((parts[0].astype(F32) + parts[1]) + (parts[2].astype(F32) + parts[3])).astype(BF)
    parts = [part] + [swap(part, "tile", step << 1) for step in range(1, 4)]
    part = ((parts[0].astype(F32) + parts[1]) + (parts[2].astype(F32) + parts[3])).astype(BF)
    shape = (DEPTH, 2, band, 2 * SIDE)
    own_grad, spill = call(gather_kernel, [(shape, F32), (shape, BF)], (which, *bands), 1)
    part, spill = lax.optimization_barrier((part, spill))
    parts = [part] + [swap(part, "tile", step << 3) for step in range(1, 4)]
    (merged,) = call(merge_kernel, [((2, half, SIDE), BF)], (which, *parts), 1)
    (probe_grad,) = call(
        finish_kernel, [((1, 2) + square, F32)], (which, merged, swap(merged, "tile", 1)), 1
    )

    object_grad = own_grad + shift(spill, "tile", 1).astype(F32)
    return (object_grad, probe_grad)


def solution(mesh):
    placed = (
        P(None, None, "tile", None),
        P("mode", None, None, None),
        P("tile", None),
        P("tile", None, None),
    )
    return jax.shard_map(
        on_device,
        mesh=mesh,
        in_specs=placed,
        out_specs=(P(None, None, ("tile", "mode"), None), P("mode", None, None, None)),
        check_vma=False,
    )
```

```python
import functools
import math

import jax
import jax.numpy as jnp
import numpy as np
from jax import lax
from jax.experimental import pallas as pl
from jax.experimental.pallas import tpu as pltpu
from jax.sharding import PartitionSpec as P

fresnel = 0.4
SIDE = 256
DEPTH = 3
SLOTS = 4
BF = jnp.bfloat16
F32 = jnp.float32
VMEM = pl.BlockSpec(memory_space=pltpu.VMEM)
HBM = pl.BlockSpec(memory_space=pltpu.HBM)
SMEM = pl.BlockSpec(memory_space=pltpu.SMEM)
PARAMS = pltpu.CompilerParams(vmem_limit_bytes=16 * 1024 * 1024)


def constants():
    index = np.arange(SIDE)
    folded = index[:, None] * index[None, :] % SIDE
    angle = np.float32(2.0 * math.pi / SIDE) * folded.astype(np.float32)
    scale = np.float32(1.0 / math.sqrt(SIDE))
    real = (np.cos(angle) * scale).astype(jnp.bfloat16)
    imag = (-np.sin(angle) * scale).astype(jnp.bfloat16)
    return np.concatenate([real, imag], 1)


def swap(block, axis, bits):
    route = [(i, i ^ bits) for i in range(lax.axis_size(axis))]
    return lax.ppermute(block, axis, route)


def shift(block, axis, distance):
    size = lax.axis_size(axis)
    return lax.ppermute(block, axis, [(i, (i + distance) % size) for i in range(size)])


def dot(first, second):
    return jnp.dot(first, second, preferred_element_type=F32)


def row_of(which, place):
    return which[4 + 2 * place]


def column_of(which, place):
    return which[5 + 2 * place]


def iotas():
    rows = lax.broadcasted_iota(jnp.int32, (SIDE, SIDE), 0)
    cols = lax.broadcasted_iota(jnp.int32, (SIDE, SIDE), 1)
    return rows, cols


def to_residues(offset):
    rows, cols = iotas()
    return jnp.where(((rows - offset) & (SIDE - 1)) == cols, 1.0, 0.0).astype(BF)


def from_residues(offset):
    rows, cols = iotas()
    return jnp.where(((cols - offset) & (SIDE - 1)) == rows, 1.0, 0.0).astype(BF)


def make_tables(which, table, row_t, row_tt, col_t, col_tt, kernel):
    place = which[1]
    offsets = (row_of(which, place), column_of(which, place))
    for offset, plain, turned in zip(offsets, (row_t, col_t), (row_tt, col_tt)):
        rolled = dot(to_residues(offset), table[...]).astype(BF)
        real, imag = rolled[:, :SIDE], rolled[:, SIDE:]
        plain[:SIDE, :SIDE] = real
        plain[:SIDE, SIDE:] = imag
        plain[SIDE:, :SIDE] = -imag
        plain[SIDE:, SIDE:] = real
        back = from_residues(offset)
        real = dot(table[:, :SIDE], back).astype(BF)
        imag = dot(table[:, SIDE:], back).astype(BF)
        turned[:SIDE, :SIDE] = real
        turned[:SIDE, SIDE:] = -imag
        turned[SIDE:, :SIDE] = imag
        turned[SIDE:, SIDE:] = real
    index = lax.broadcasted_iota(jnp.int32, (8, SIDE), 1)
    freq = (((index + SIDE // 2) & (SIDE - 1)) - SIDE // 2).astype(F32)
    phase = freq * freq * (-math.pi * fresnel / SIDE)
    cos_row = jnp.broadcast_to(jnp.cos(phase)[:1], (SIDE, SIDE))
    sin_row = jnp.broadcast_to(jnp.sin(phase)[:1], (SIDE, SIDE))
    cos_col, sin_col = cos_row.T, sin_row.T
    kernel[0] = cos_col * cos_row - sin_col * sin_row
    kernel[1] = cos_col * sin_row + sin_col * cos_row


def fill(field, slot, real, imag):
    field[slot, :SIDE, :] = real.astype(BF)
    field[slot, SIDE:, :] = imag.astype(BF)


def transform(field, mid, slot, left, right):
    turned = dot(left[...], field[slot])
    mid[slot, :, :SIDE] = turned[:SIDE].astype(BF)
    mid[slot, :, SIDE:] = turned[SIDE:].astype(BF)
    out = dot(mid[slot], right[...])
    return out[:, :SIDE], out[:, SIDE:]


def transform_all(field, mid, slots, left, right, store):
    for slot in range(slots):
        store(slot, *transform(field, mid, slot, left, right))


def propagate_all(field, mid, slots, forth, back, kernel, sign, store):
    def turn(slot, real, imag):
        turned = sign * kernel[1]
        fill(field, slot, real * kernel[0] - imag * turned, real * turned + imag * kernel[0])

    transform_all(field, mid, slots, *forth, turn)
    transform_all(field, mid, slots, *back, store)


def choose_kernel(which, above, strip, *outs):
    cols = lax.broadcasted_iota(jnp.int32, (SIDE, SIDE), 1)
    on_left = cols >= above[which[1], 1]
    part = which[0] >> 2
    for layer, out in enumerate(outs):
        value = strip[layer, part].astype(F32)
        out[...] = jnp.where(on_left, value[:, :SIDE], value[:, SIDE:]).astype(BF)


def prepare_kernel(which, table, strip, row_t, row_tt, col_t, col_tt, kernel, picked):
    make_tables(which, table, row_t, row_tt, col_t, col_tt, kernel)
    cols = lax.broadcasted_iota(jnp.int32, (SIDE, SIDE), 1)
    on_left = cols >= column_of(which, which[1])
    for layer in range(DEPTH):
        for part in range(2):
            value = strip[layer, part].astype(F32)
            picked[layer, part] = jnp.where(on_left, value[:, :SIDE], value[:, SIDE:]).astype(BF)


def forward_kernel(layer, which, picked, mine, other, *refs):
    row_t, row_tt, col_t, col_tt, kernel, *refs = refs
    rows, cols = iotas()
    on_strip = rows >= row_of(which, which[1])
    if layer == 0:
        probe, one, two_real, two_imag, three, window, wave, *outs, field, mid = refs
        there = to_residues(row_of(which, which[1]))
        back = from_residues(column_of(which, which[1]))
        sources = (probe[0], probe[1], one[0], one[1], two_real[...], two_imag[...])
        for index, source in enumerate(sources + (three[0], three[1])):
            moved = dot(there, source).astype(BF)
            wave[index // 2, index % 2] = dot(moved, back).astype(BF)
    else:
        wave, window, *outs, field, mid = refs
    for part in range(2):
        have = (which[0] >> 2) == part
        below = jnp.where(have, mine[...].astype(F32), other[...].astype(F32))
        above = picked[layer, part].astype(F32)
        window[part] = jnp.where(on_strip, above, below).astype(BF)
    forth = (row_tt, col_t)
    back = (row_t, col_tt)
    for slot in range(SLOTS):
        obj_real = window[0].astype(F32)
        obj_imag = window[1].astype(F32)
        real = wave[slot, 0].astype(F32)
        imag = wave[slot, 1].astype(F32)
        fill(field, slot, real * obj_real - imag * obj_imag, real * obj_imag + imag * obj_real)
    if layer + 1 < DEPTH:
        (wave_out,) = outs

        def store(slot, real, imag):
            wave_out[slot, 0] = real.astype(BF)
            wave_out[slot, 1] = imag.astype(BF)

        propagate_all(field, mid, SLOTS, forth, back, kernel, 1.0, store)
    else:
        far, total, total_sent = outs

        def store_far(slot, real, imag):
            far[slot, 0] = real
            far[slot, 1] = imag
            power = real * real + imag * imag
            total[...] = power if slot == 0 else total[...] + power

        transform_all(field, mid, SLOTS, *forth, store_far)
        total_sent[...] = total[...].astype(BF)


def backward_kernel(
    which, window0, window1, window2, wave0, wave1, wave2, far, total, total_got,
    row_t, row_tt, col_t, col_tt, kernel, measured_hbm,
    grad_keep, grad_send, keep_out, send_out, field, mid, residual, grads, sums, backs, measured, sem,
):
    place = which[1]
    copy = pltpu.make_async_copy(measured_hbm.at[place], measured, sem)
    copy.start()
    row, col = row_of(which, place), column_of(which, place)
    copy.wait()
    residual[...] = total[...] + total_got[...].astype(F32) - measured[...]
    forth = (row_tt, col_t)
    back = (row_t, col_tt)
    waves = (wave0, wave1, wave2)
    windows = (window0, window1, window2)

    def store(slot, real, imag):
        backs[slot, 0] = real.astype(BF)
        backs[slot, 1] = imag.astype(BF)

    for slot in range(SLOTS):
        fill(field, slot, residual[...] * far[slot, 0], residual[...] * far[slot, 1])
    transform_all(field, mid, SLOTS, *back, store)
    for layer in reversed(range(DEPTH)):
        for slot in range(SLOTS):
            gin_real = backs[slot, 0].astype(F32)
            gin_imag = backs[slot, 1].astype(F32)
            real = waves[layer][slot, 0].astype(F32)
            imag = waves[layer][slot, 1].astype(F32)
            grad_real = real * gin_real + imag * gin_imag
            grad_imag = real * gin_imag - imag * gin_real
            if slot > 0:
                grad_real += grads[0]
                grad_imag += grads[1]
            if slot + 1 < SLOTS:
                grads[0] = grad_real
                grads[1] = grad_imag
            else:
                sums[layer, 0] = grad_real.astype(BF)
                sums[layer, 1] = grad_imag.astype(BF)
            obj_real = windows[layer][0].astype(F32)
            obj_imag = windows[layer][1].astype(F32)
            next_real = obj_real * gin_real + obj_imag * gin_imag
            next_imag = obj_real * gin_imag - obj_imag * gin_real
            fill(field, slot, next_real, next_imag)
        if layer > 0:
            propagate_all(field, mid, SLOTS, forth, back, kernel, -1.0, store)
    rows = from_residues(row)
    cols = to_residues(col)
    for slot in range(SLOTS):
        for part in range(2):
            moved = dot(rows, field[slot, part * SIDE : (part + 1) * SIDE, :]).astype(BF)
            backs[slot, part] = dot(moved, cols).astype(BF)
    half = SIDE // 2
    kept = pl.multiple_of((which[0] >> 2) * half, half)
    sent = pl.multiple_of(half - kept, half)
    grad_keep[...] = sums[:, :, pl.ds(kept, half), :]
    grad_send[...] = sums[:, :, pl.ds(sent, half), :]
    kept = pl.multiple_of(which[2] * half, half)
    sent = pl.multiple_of(half - kept, half)
    keep_out[...] = backs[:, :, pl.ds(kept, half), :]
    send_out[...] = backs[:, :, pl.ds(sent, half), :]


def pair_kernel(which, keep, got, own_out, *outs):
    band = SIDE // 8
    for step in range(SLOTS):
        part = pl.ds(pl.multiple_of((which[1] ^ step) * band, band), band)
        for layer in range(DEPTH):
            for side in range(2):
                value = keep[layer, side, part, :].astype(F32) + got[layer, side, part, :].astype(F32)
                if step == 0:
                    own_out[layer, side] = value
                else:
                    outs[step - 1][layer, side] = value.astype(BF)


def gather_kernel(which, own, got1, got2, got3, own_out, spill_out):
    band = SIDE // 8
    top = which[0] * band
    shape = (band, SIDE)
    rows = lax.broadcasted_iota(jnp.int32, shape, 0) + top
    cols = lax.broadcasted_iota(jnp.int32, shape, 1)
    for layer in range(DEPTH):
        for part in range(2):
            sums = [jnp.zeros(shape, F32) for _ in range(4)]
            for step, grads in enumerate((own, got1, got2, got3)):
                value = grads[layer, part].astype(F32)
                place = which[1] ^ step
                on_strip = rows >= row_of(which, place)
                on_left = cols >= column_of(which, place)
                for index, (here, left) in enumerate(
                    ((True, True), (True, False), (False, True), (False, False))
                ):
                    picked = on_strip if here else ~on_strip
                    picked &= on_left if left else ~on_left
                    sums[index] += jnp.where(picked, value, 0.0)
            own_out[layer, part, :, :SIDE] = sums[0]
            own_out[layer, part, :, SIDE:] = sums[1]
            spill_out[layer, part, :, :SIDE] = sums[2].astype(BF)
            spill_out[layer, part, :, SIDE:] = sums[3].astype(BF)


def first_kernel(keep, got, own, sent_one, sent_three):
    for slot in range(SLOTS):
        for part in range(2):
            total = (keep[slot, part].astype(F32) + got[slot, part].astype(F32)).astype(BF)
            if part == 0 and slot in (1, 2):
                sent_one[slot - 1] = total
            elif part == 1 and slot in (2, 3):
                sent_three[3 - slot] = total
            else:
                own[slot if slot == 0 else 1, part] = total


def second_kernel(own, got_one, got_three, held, sent_three, sent_one):
    for part, got, sent in ((0, got_one, sent_three), (1, got_three, sent_one)):
        held[part] = own[0, part].astype(F32) + got[0].astype(F32)
        sent[...] = (own[1, part].astype(F32) + got[1].astype(F32)).astype(BF)


def quarter_kernel(which, held, got_three, got_one, *outs):
    scratch = outs[-1]
    scratch[0] = (held[0] + got_three[...].astype(F32)).astype(BF)
    scratch[1] = (held[1] + got_one[...].astype(F32)).astype(BF)
    depth = scratch.shape[1] // 4
    for step in range(4):
        top = pl.multiple_of((which[3] ^ step) * depth, depth)
        outs[step][...] = scratch[:, pl.ds(top, depth), :]


def merge_kernel(which, part0, part1, part2, part3, out):
    depth = part0.shape[1]
    for step, part in enumerate((part0, part1, part2, part3)):
        top = pl.multiple_of((which[3] ^ step) * depth, depth)
        out[:, pl.ds(top, depth), :] = part[...]


def finish_kernel(which, own, got, out):
    half = SIDE // 2
    kept = pl.multiple_of(which[2] * half, half)
    out[0, :, pl.ds(kept, half), :] = own[...].astype(F32)
    out[0, :, pl.ds(pl.multiple_of(half - kept, half), half), :] = got[...].astype(F32)


def call(kernel, outs, arguments, scalars, scratch=()):
    return pl.pallas_call(
        kernel,
        out_shape=[jax.ShapeDtypeStruct(shape, dtype) for shape, dtype in outs],
        in_specs=[SMEM] * scalars + [VMEM] * (len(arguments) - scalars),
        out_specs=[VMEM] * len(outs),
        scratch_shapes=[pltpu.VMEM(shape, dtype) for shape, dtype in scratch],
        compiler_params=PARAMS,
    )(*arguments)


def on_device(object_slices, probe_modes, positions, measured):
    tile = lax.axis_index("tile")
    mode = lax.axis_index("mode")
    place = mode & (SLOTS - 1)
    which = jnp.stack([mode, place, tile & 1, tile >> 3]).astype(jnp.int32)
    which = jnp.concatenate([which, positions.reshape(-1)])
    half = SIDE // 2
    band = SIDE // 8
    square = (SIDE, SIDE)
    wide = (2 * SIDE, 2 * SIDE)
    table = jnp.asarray(constants())

    slots = (SLOTS, 2) + square
    layers = (DEPTH, 2) + square
    pair_of = ((2,) + square, BF)
    above = shift(positions, "tile", 1)
    *tables, picked = call(
        prepare_kernel,
        [(wide, BF)] * 4 + [((2,) + square, F32), (layers, BF)],
        (which, table, object_slices),
        1,
    )
    above, probe = lax.optimization_barrier((above, probe_modes[0]))
    chosen = call(choose_kernel, [(square, BF)] * DEPTH, (which, above, object_slices), 2)
    mine = [shift(part, "tile", -1) for part in chosen]
    one, three = (swap(probe, "mode", step) for step in (1, 3))
    mine[0], one, three, picked = lax.optimization_barrier((mine[0], one, three, picked))
    two = [swap(three[0], "mode", 1), swap(one[1], "mode", 3)]
    other = [swap(part, "mode", 4) for part in mine]

    scratch = [((SLOTS, 2 * SIDE, SIDE), BF), ((SLOTS, SIDE, 2 * SIDE), BF)]
    windows = []
    waves = []
    for layer in range(DEPTH):
        common = (which, picked, mine[layer], other[layer], *tables)
        if layer == 0:
            given = (probe_modes[0], one, *two, three)
            outs = [pair_of, (slots, BF), (slots, BF)]
        elif layer + 1 < DEPTH:
            given = (waves[layer],)
            outs = [pair_of, (slots, BF)]
        else:
            given = (waves[layer],)
            outs = [pair_of, (slots, F32), (square, F32), (square, BF)]
        kernel = functools.partial(forward_kernel, layer)
        window, *results = call(kernel, outs, common + given, 1, scratch)
        windows.append(window)
        if layer + 1 < DEPTH:
            waves += results
    far, total, total_sent = results
    total_got = swap(total_sent, "mode", 4)
    piece = ((SLOTS, 2, half, SIDE), BF)
    outs = [((DEPTH, 2, half, SIDE), BF)] * 2 + [piece, piece]
    scratch += [(square, F32), ((2,) + square, F32), (layers, BF), (slots, BF), (square, F32)]
    grad_keep, grad_send, keep, send = pl.pallas_call(
        backward_kernel,
        out_shape=[jax.ShapeDtypeStruct(*out) for out in outs],
        in_specs=[SMEM] + [VMEM] * 14 + [HBM],
        out_specs=[VMEM] * 4,
        scratch_shapes=[pltpu.VMEM(*shape) for shape in scratch] + [pltpu.SemaphoreType.DMA],
        compiler_params=PARAMS,
    )(which, *windows, *waves, far, total, total_got, *tables, measured)

    grad_got = swap(grad_send, "mode", 4)

    pair = ((2, half, SIDE), BF)
    own, sent_one, sent_three = call(
        first_kernel, [((2,) + pair[0], BF), pair, pair], (keep, swap(send, "tile", 1)), 0
    )
    held, sent_three, sent_one = call(
        second_kernel,
        [(pair[0], F32), ((half, SIDE), BF), ((half, SIDE), BF)],
        (own, swap(sent_one, "mode", 1), swap(sent_three, "mode", 3)),
        0,
    )
    grad_got, held = lax.optimization_barrier((grad_got, held))
    shape = (DEPTH, 2, band, SIDE)
    bands = call(
        pair_kernel, [(shape, F32)] + [(shape, BF)] * 3, (which, grad_keep, grad_got), 1
    )
    bands, held = lax.optimization_barrier((bands, held))
    quarters = call(
        quarter_kernel,
        [((2, half // 4, SIDE), BF)] * 4,
        (which, held, swap(sent_three, "mode", 3), swap(sent_one, "mode", 1)),
        1,
        [pair],
    )
    parts = [quarters[0]] + [swap(quarters[step], "tile", step << 3) for step in range(1, 4)]
    bands = [bands[0]] + [swap(bands[step], "mode", step) for step in range(1, 4)]
    bands, parts = lax.optimization_barrier((bands, parts))
    part = ((parts[0].astype(F32) + parts[1]) + (parts[2].astype(F32) + parts[3])).astype(BF)
    parts = [part] + [swap(part, "tile", step << 1) for step in range(1, 4)]
    part = ((parts[0].astype(F32) + parts[1]) + (parts[2].astype(F32) + parts[3])).astype(BF)
    shape = (DEPTH, 2, band, 2 * SIDE)
    own_grad, spill = call(gather_kernel, [(shape, F32), (shape, BF)], (which, *bands), 1)
    part, spill = lax.optimization_barrier((part, spill))
    parts = [part] + [swap(part, "tile", step << 3) for step in range(1, 4)]
    (merged,) = call(merge_kernel, [((2, half, SIDE), BF)], (which, *parts), 1)
    (probe_grad,) = call(
        finish_kernel, [((1, 2) + square, F32)], (which, merged, swap(merged, "tile", 1)), 1
    )

    object_grad = own_grad + shift(spill, "tile", 1).astype(F32)
    return (object_grad, probe_grad)


def solution(mesh):
    placed = (
        P(None, None, "tile", None),
        P("mode", None, None, None),
        P("tile", None),
        P("tile", None, None),
    )
    return jax.shard_map(
        on_device,
        mesh=mesh,
        in_specs=placed,
        out_specs=(P(None, None, ("tile", "mode"), None), P("mode", None, None, None)),
        check_vma=False,
    )
```

```python
import functools
import math

import jax
import jax.numpy as jnp
import numpy as np
from jax import lax
from jax.experimental import pallas as pl
from jax.experimental.pallas import tpu as pltpu
from jax.sharding import PartitionSpec as P

fresnel = 0.4
SIDE = 256
DEPTH = 3
SLOTS = 4
BF = jnp.bfloat16
F32 = jnp.float32
VMEM = pl.BlockSpec(memory_space=pltpu.VMEM)
HBM = pl.BlockSpec(memory_space=pltpu.HBM)
SMEM = pl.BlockSpec(memory_space=pltpu.SMEM)
PARAMS = pltpu.CompilerParams(vmem_limit_bytes=16 * 1024 * 1024)


def constants():
    index = np.arange(SIDE)
    folded = index[:, None] * index[None, :] % SIDE
    angle = np.float32(2.0 * math.pi / SIDE) * folded.astype(np.float32)
    scale = np.float32(1.0 / math.sqrt(SIDE))
    real = (np.cos(angle) * scale).astype(jnp.bfloat16)
    imag = (-np.sin(angle) * scale).astype(jnp.bfloat16)
    return np.concatenate([real, imag], 1)


def swap(block, axis, bits):
    route = [(i, i ^ bits) for i in range(lax.axis_size(axis))]
    return lax.ppermute(block, axis, route)


def shift(block, axis, distance):
    size = lax.axis_size(axis)
    return lax.ppermute(block, axis, [(i, (i + distance) % size) for i in range(size)])


def dot(first, second):
    return jnp.dot(first, second, preferred_element_type=F32)


def row_of(which, place):
    return which[4 + 2 * place]


def column_of(which, place):
    return which[5 + 2 * place]


def iotas():
    rows = lax.broadcasted_iota(jnp.int32, (SIDE, SIDE), 0)
    cols = lax.broadcasted_iota(jnp.int32, (SIDE, SIDE), 1)
    return rows, cols


def to_residues(offset):
    rows, cols = iotas()
    return jnp.where(((rows - offset) & (SIDE - 1)) == cols, 1.0, 0.0).astype(BF)


def from_residues(offset):
    rows, cols = iotas()
    return jnp.where(((cols - offset) & (SIDE - 1)) == rows, 1.0, 0.0).astype(BF)


def make_tables(which, table, row_t, row_tt, col_t, col_tt, kernel):
    place = which[1]
    offsets = (row_of(which, place), column_of(which, place))
    for offset, plain, turned in zip(offsets, (row_t, col_t), (row_tt, col_tt)):
        rolled = dot(to_residues(offset), table[...]).astype(BF)
        real, imag = rolled[:, :SIDE], rolled[:, SIDE:]
        plain[:SIDE, :SIDE] = real
        plain[:SIDE, SIDE:] = imag
        plain[SIDE:, :SIDE] = -imag
        plain[SIDE:, SIDE:] = real
        back = from_residues(offset)
        real = dot(table[:, :SIDE], back).astype(BF)
        imag = dot(table[:, SIDE:], back).astype(BF)
        turned[:SIDE, :SIDE] = real
        turned[:SIDE, SIDE:] = -imag
        turned[SIDE:, :SIDE] = imag
        turned[SIDE:, SIDE:] = real
    index = lax.broadcasted_iota(jnp.int32, (8, SIDE), 1)
    freq = (((index + SIDE // 2) & (SIDE - 1)) - SIDE // 2).astype(F32)
    phase = freq * freq * (-math.pi * fresnel / SIDE)
    cos_row = jnp.broadcast_to(jnp.cos(phase)[:1], (SIDE, SIDE))
    sin_row = jnp.broadcast_to(jnp.sin(phase)[:1], (SIDE, SIDE))
    cos_col, sin_col = cos_row.T, sin_row.T
    kernel[0] = cos_col * cos_row - sin_col * sin_row
    kernel[1] = cos_col * sin_row + sin_col * cos_row


def fill(field, slot, real, imag):
    field[slot, :SIDE, :] = real.astype(BF)
    field[slot, SIDE:, :] = imag.astype(BF)


def transform(field, mid, slot, left, right):
    turned = dot(left[...], field[slot])
    mid[slot, :, :SIDE] = turned[:SIDE].astype(BF)
    mid[slot, :, SIDE:] = turned[SIDE:].astype(BF)
    out = dot(mid[slot], right[...])
    return out[:, :SIDE], out[:, SIDE:]


def transform_all(field, mid, slots, left, right, store):
    for slot in range(slots):
        store(slot, *transform(field, mid, slot, left, right))


def propagate_all(field, mid, slots, forth, back, kernel, sign, store):
    def turn(slot, real, imag):
        turned = sign * kernel[1]
        fill(field, slot, real * kernel[0] - imag * turned, real * turned + imag * kernel[0])

    transform_all(field, mid, slots, *forth, turn)
    transform_all(field, mid, slots, *back, store)


def choose_kernel(which, above, strip, *outs):
    cols = lax.broadcasted_iota(jnp.int32, (SIDE, SIDE), 1)
    on_left = cols >= above[which[1], 1]
    part = which[0] >> 2
    for layer, out in enumerate(outs):
        value = strip[layer, part].astype(F32)
        out[...] = jnp.where(on_left, value[:, :SIDE], value[:, SIDE:]).astype(BF)


def prepare_kernel(which, table, strip, row_t, row_tt, col_t, col_tt, kernel, picked):
    make_tables(which, table, row_t, row_tt, col_t, col_tt, kernel)
    cols = lax.broadcasted_iota(jnp.int32, (SIDE, SIDE), 1)
    on_left = cols >= column_of(which, which[1])
    for layer in range(DEPTH):
        for part in range(2):
            value = strip[layer, part].astype(F32)
            picked[layer, part] = jnp.where(on_left, value[:, :SIDE], value[:, SIDE:]).astype(BF)


def forward_kernel(layer, which, picked, mine, other, *refs):
    row_t, row_tt, col_t, col_tt, kernel, *refs = refs
    rows, cols = iotas()
    on_strip = rows >= row_of(which, which[1])
    if layer == 0:
        probe, one, two_real, two_imag, three, window, wave, *outs, field, mid = refs
        there = to_residues(row_of(which, which[1]))
        back = from_residues(column_of(which, which[1]))
        sources = (probe[0], probe[1], one[0], one[1], two_real[...], two_imag[...])
        for index, source in enumerate(sources + (three[0], three[1])):
            moved = dot(there, source).astype(BF)
            wave[index // 2, index % 2] = dot(moved, back).astype(BF)
    else:
        wave, window, *outs, field, mid = refs
    for part in range(2):
        have = (which[0] >> 2) == part
        below = jnp.where(have, mine[...].astype(F32), other[...].astype(F32))
        above = picked[layer, part].astype(F32)
        window[part] = jnp.where(on_strip, above, below).astype(BF)
    forth = (row_tt, col_t)
    back = (row_t, col_tt)
    for slot in range(SLOTS):
        obj_real = window[0].astype(F32)
        obj_imag = window[1].astype(F32)
        real = wave[slot, 0].astype(F32)
        imag = wave[slot, 1].astype(F32)
        fill(field, slot, real * obj_real - imag * obj_imag, real * obj_imag + imag * obj_real)
    if layer + 1 < DEPTH:
        (wave_out,) = outs

        def store(slot, real, imag):
            wave_out[slot, 0] = real.astype(BF)
            wave_out[slot, 1] = imag.astype(BF)

        propagate_all(field, mid, SLOTS, forth, back, kernel, 1.0, store)
    else:
        far, total, total_sent = outs

        def store_far(slot, real, imag):
            far[slot, 0] = real
            far[slot, 1] = imag
            power = real * real + imag * imag
            total[...] = power if slot == 0 else total[...] + power

        transform_all(field, mid, SLOTS, *forth, store_far)
        total_sent[...] = total[...].astype(BF)


def backward_kernel(
    which, window0, window1, window2, wave0, wave1, wave2, far, total, total_got,
    row_t, row_tt, col_t, col_tt, kernel, measured_hbm,
    grad_keep, grad_send, keep_out, send_out, field, mid, residual, grads, sums, backs, measured, sem,
):
    place = which[1]
    copy = pltpu.make_async_copy(measured_hbm.at[place], measured, sem)
    copy.start()
    row, col = row_of(which, place), column_of(which, place)
    copy.wait()
    residual[...] = total[...] + total_got[...].astype(F32) - measured[...]
    forth = (row_tt, col_t)
    back = (row_t, col_tt)
    waves = (wave0, wave1, wave2)
    windows = (window0, window1, window2)

    def store(slot, real, imag):
        backs[slot, 0] = real.astype(BF)
        backs[slot, 1] = imag.astype(BF)

    for slot in range(SLOTS):
        fill(field, slot, residual[...] * far[slot, 0], residual[...] * far[slot, 1])
    transform_all(field, mid, SLOTS, *back, store)
    for layer in reversed(range(DEPTH)):
        for slot in range(SLOTS):
            gin_real = backs[slot, 0].astype(F32)
            gin_imag = backs[slot, 1].astype(F32)
            real = waves[layer][slot, 0].astype(F32)
            imag = waves[layer][slot, 1].astype(F32)
            grad_real = real * gin_real + imag * gin_imag
            grad_imag = real * gin_imag - imag * gin_real
            if slot > 0:
                grad_real += grads[0]
                grad_imag += grads[1]
            if slot + 1 < SLOTS:
                grads[0] = grad_real
                grads[1] = grad_imag
            else:
                sums[layer, 0] = grad_real.astype(BF)
                sums[layer, 1] = grad_imag.astype(BF)
            obj_real = windows[layer][0].astype(F32)
            obj_imag = windows[layer][1].astype(F32)
            next_real = obj_real * gin_real + obj_imag * gin_imag
            next_imag = obj_real * gin_imag - obj_imag * gin_real
            fill(field, slot, next_real, next_imag)
        if layer > 0:
            propagate_all(field, mid, SLOTS, forth, back, kernel, -1.0, store)
    rows = from_residues(row)
    cols = to_residues(col)
    for slot in range(SLOTS):
        for part in range(2):
            moved = dot(rows, field[slot, part * SIDE : (part + 1) * SIDE, :]).astype(BF)
            backs[slot, part] = dot(moved, cols).astype(BF)
    half = SIDE // 2
    kept = pl.multiple_of((which[0] >> 2) * half, half)
    sent = pl.multiple_of(half - kept, half)
    grad_keep[...] = sums[:, :, pl.ds(kept, half), :]
    grad_send[...] = sums[:, :, pl.ds(sent, half), :]
    kept = pl.multiple_of(which[2] * half, half)
    sent = pl.multiple_of(half - kept, half)
    keep_out[...] = backs[:, :, pl.ds(kept, half), :]
    send_out[...] = backs[:, :, pl.ds(sent, half), :]


def pair_kernel(which, keep, got, own_out, *outs):
    band = SIDE // 8
    for step in range(SLOTS):
        part = pl.ds(pl.multiple_of((which[1] ^ step) * band, band), band)
        for layer in range(DEPTH):
            for side in range(2):
                value = keep[layer, side, part, :].astype(F32) + got[layer, side, part, :].astype(F32)
                if step == 0:
                    own_out[layer, side] = value
                else:
                    outs[step - 1][layer, side] = value.astype(BF)


def gather_kernel(which, own, got1, got2, got3, own_out, spill_out):
    band = SIDE // 8
    top = which[0] * band
    shape = (band, SIDE)
    rows = lax.broadcasted_iota(jnp.int32, shape, 0) + top
    cols = lax.broadcasted_iota(jnp.int32, shape, 1)
    for layer in range(DEPTH):
        for part in range(2):
            sums = [jnp.zeros(shape, F32) for _ in range(4)]
            for step, grads in enumerate((own, got1, got2, got3)):
                value = grads[layer, part].astype(F32)
                place = which[1] ^ step
                on_strip = rows >= row_of(which, place)
                on_left = cols >= column_of(which, place)
                for index, (here, left) in enumerate(
                    ((True, True), (True, False), (False, True), (False, False))
                ):
                    picked = on_strip if here else ~on_strip
                    picked &= on_left if left else ~on_left
                    sums[index] += jnp.where(picked, value, 0.0)
            own_out[layer, part, :, :SIDE] = sums[0]
            own_out[layer, part, :, SIDE:] = sums[1]
            spill_out[layer, part, :, :SIDE] = sums[2].astype(BF)
            spill_out[layer, part, :, SIDE:] = sums[3].astype(BF)


def first_kernel(keep, got, own, sent_one, sent_three):
    for slot in range(SLOTS):
        for part in range(2):
            total = (keep[slot, part].astype(F32) + got[slot, part].astype(F32)).astype(BF)
            if part == 0 and slot in (1, 2):
                sent_one[slot - 1] = total
            elif part == 1 and slot in (2, 3):
                sent_three[3 - slot] = total
            else:
                own[slot if slot == 0 else 1, part] = total


def second_kernel(own, got_one, got_three, held, sent_three, sent_one):
    for part, got, sent in ((0, got_one, sent_three), (1, got_three, sent_one)):
        held[part] = own[0, part].astype(F32) + got[0].astype(F32)
        sent[...] = (own[1, part].astype(F32) + got[1].astype(F32)).astype(BF)


def quarter_kernel(which, held, got_three, got_one, *outs):
    scratch = outs[-1]
    scratch[0] = (held[0] + got_three[...].astype(F32)).astype(BF)
    scratch[1] = (held[1] + got_one[...].astype(F32)).astype(BF)
    depth = scratch.shape[1] // 4
    for step in range(4):
        top = pl.multiple_of((which[3] ^ step) * depth, depth)
        outs[step][...] = scratch[:, pl.ds(top, depth), :]


def merge_kernel(which, part0, part1, part2, part3, out):
    depth = part0.shape[1]
    for step, part in enumerate((part0, part1, part2, part3)):
        top = pl.multiple_of((which[3] ^ step) * depth, depth)
        out[:, pl.ds(top, depth), :] = part[...]


def finish_kernel(which, own, got, out):
    half = SIDE // 2
    kept = pl.multiple_of(which[2] * half, half)
    out[0, :, pl.ds(kept, half), :] = own[...].astype(F32)
    out[0, :, pl.ds(pl.multiple_of(half - kept, half), half), :] = got[...].astype(F32)


def call(kernel, outs, arguments, scalars, scratch=()):
    return pl.pallas_call(
        kernel,
        out_shape=[jax.ShapeDtypeStruct(shape, dtype) for shape, dtype in outs],
        in_specs=[SMEM] * scalars + [VMEM] * (len(arguments) - scalars),
        out_specs=[VMEM] * len(outs),
        scratch_shapes=[pltpu.VMEM(shape, dtype) for shape, dtype in scratch],
        compiler_params=PARAMS,
    )(*arguments)


def on_device(object_slices, probe_modes, positions, measured):
    tile = lax.axis_index("tile")
    mode = lax.axis_index("mode")
    place = mode & (SLOTS - 1)
    which = jnp.stack([mode, place, tile & 1, tile >> 3]).astype(jnp.int32)
    which = jnp.concatenate([which, positions.reshape(-1)])
    half = SIDE // 2
    band = SIDE // 8
    square = (SIDE, SIDE)
    wide = (2 * SIDE, 2 * SIDE)
    table = jnp.asarray(constants())

    slots = (SLOTS, 2) + square
    layers = (DEPTH, 2) + square
    pair_of = ((2,) + square, BF)
    above = shift(positions, "tile", 1)
    *tables, picked = call(
        prepare_kernel,
        [(wide, BF)] * 4 + [((2,) + square, F32), (layers, BF)],
        (which, table, object_slices),
        1,
    )
    above, probe, picked = lax.optimization_barrier((above, probe_modes[0], picked))
    chosen = call(choose_kernel, [(square, BF)] * DEPTH, (which, above, object_slices), 2)
    mine = [shift(part, "tile", -1) for part in chosen]
    one, three = (swap(probe, "mode", step) for step in (1, 3))
    mine[0], one, three = lax.optimization_barrier((mine[0], one, three))
    two = [swap(three[0], "mode", 1), swap(one[1], "mode", 3)]
    other = [swap(part, "mode", 4) for part in mine]

    scratch = [((SLOTS, 2 * SIDE, SIDE), BF), ((SLOTS, SIDE, 2 * SIDE), BF)]
    windows = []
    waves = []
    for layer in range(DEPTH):
        common = (which, picked, mine[layer], other[layer], *tables)
        if layer == 0:
            given = (probe_modes[0], one, *two, three)
            outs = [pair_of, (slots, BF), (slots, BF)]
        elif layer + 1 < DEPTH:
            given = (waves[layer],)
            outs = [pair_of, (slots, BF)]
        else:
            given = (waves[layer],)
            outs = [pair_of, (slots, F32), (square, F32), (square, BF)]
        kernel = functools.partial(forward_kernel, layer)
        window, *results = call(kernel, outs, common + given, 1, scratch)
        windows.append(window)
        if layer + 1 < DEPTH:
            waves += results
    far, total, total_sent = results
    total_got = swap(total_sent, "mode", 4)
    piece = ((SLOTS, 2, half, SIDE), BF)
    outs = [((DEPTH, 2, half, SIDE), BF)] * 2 + [piece, piece]
    scratch += [(square, F32), ((2,) + square, F32), (layers, BF), (slots, BF), (square, F32)]
    grad_keep, grad_send, keep, send = pl.pallas_call(
        backward_kernel,
        out_shape=[jax.ShapeDtypeStruct(*out) for out in outs],
        in_specs=[SMEM] + [VMEM] * 14 + [HBM],
        out_specs=[VMEM] * 4,
        scratch_shapes=[pltpu.VMEM(*shape) for shape in scratch] + [pltpu.SemaphoreType.DMA],
        compiler_params=PARAMS,
    )(which, *windows, *waves, far, total, total_got, *tables, measured)

    grad_got = swap(grad_send, "mode", 4)

    pair = ((2, half, SIDE), BF)
    own, sent_one, sent_three = call(
        first_kernel, [((2,) + pair[0], BF), pair, pair], (keep, swap(send, "tile", 1)), 0
    )
    held, sent_three, sent_one = call(
        second_kernel,
        [(pair[0], F32), ((half, SIDE), BF), ((half, SIDE), BF)],
        (own, swap(sent_one, "mode", 1), swap(sent_three, "mode", 3)),
        0,
    )
    grad_got, held = lax.optimization_barrier((grad_got, held))
    shape = (DEPTH, 2, band, SIDE)
    bands = call(
        pair_kernel, [(shape, F32)] + [(shape, BF)] * 3, (which, grad_keep, grad_got), 1
    )
    bands, held = lax.optimization_barrier((bands, held))
    quarters = call(
        quarter_kernel,
        [((2, half // 4, SIDE), BF)] * 4,
        (which, held, swap(sent_three, "mode", 3), swap(sent_one, "mode", 1)),
        1,
        [pair],
    )
    parts = [quarters[0]] + [swap(quarters[step], "tile", step << 3) for step in range(1, 4)]
    bands = [bands[0]] + [swap(bands[step], "mode", step) for step in range(1, 4)]
    bands, parts = lax.optimization_barrier((bands, parts))
    part = ((parts[0].astype(F32) + parts[1]) + (parts[2].astype(F32) + parts[3])).astype(BF)
    parts = [part] + [swap(part, "tile", step << 1) for step in range(1, 4)]
    part = ((parts[0].astype(F32) + parts[1]) + (parts[2].astype(F32) + parts[3])).astype(BF)
    shape = (DEPTH, 2, band, 2 * SIDE)
    own_grad, spill = call(gather_kernel, [(shape, F32), (shape, BF)], (which, *bands), 1)
    part, spill = lax.optimization_barrier((part, spill))
    parts = [part] + [swap(part, "tile", step << 3) for step in range(1, 4)]
    (merged,) = call(merge_kernel, [((2, half, SIDE), BF)], (which, *parts), 1)
    (probe_grad,) = call(
        finish_kernel, [((1, 2) + square, F32)], (which, merged, swap(merged, "tile", 1)), 1
    )

    object_grad = own_grad + shift(spill, "tile", 1).astype(F32)
    return (object_grad, probe_grad)


def solution(mesh):
    placed = (
        P(None, None, "tile", None),
        P("mode", None, None, None),
        P("tile", None),
        P("tile", None, None),
    )
    return jax.shard_map(
        on_device,
        mesh=mesh,
        in_specs=placed,
        out_specs=(P(None, None, ("tile", "mode"), None), P("mode", None, None, None)),
        check_vma=False,
    )
```
